32 devices in a mesh: grid: 8 (over y, x, core), pair: 4 (over z).
Axes of the slice: x: 2, y: 2, z: 4, core: 2. Of those that a mesh axis runs over, the one named last changes fastest.
Arguments:
- orbitals: bfloat16 [64, 16, 4096], P('grid', None, 'pair'), may hold values from -6 to 6
- box_list: int32 [8, 4, 4], replicated, may hold values from 0 to 15, all different within a row
- pair_slots: int32 [8, 4, 4, 2], P('grid', 'pair'), may hold values from 0 to 3, as said below
- offsets: int32 [8, 4, 4, 3], P('grid', 'pair'), may hold values from -8 to 8
- pair_count: int32 [8, 4], P('grid', 'pair'), may hold values from 2 to 4, as said below
Outputs:
- exchange_field: float32 [64, 16, 4096], P('grid', None, 'pair')
The draws below stay inside these ranges and needn't reach their ends.
Inputs may be any that keep to these rules, and one draw needn't show every extreme that they name: `box_list`: the 4 orbitals of one worker's list are all different. `pair_slots`: only the first pair_count entries of a worker's lists are used; the first 2 pairs of every worker name each slot of its list exactly once. `pair_count`: each group of 4 workers that share a grid index holds 12 pairs, and one of them holds 4.
All inputs are finite; a program needn't handle non-finite values.
Results may differ from the reference program's by a relative error of at most 0.0019.
Values may be sent and summed in bfloat16 or wider, within the bound.
No kernel may reach another device: no remote copies, remote signals or barrier semaphores. Data moves between devices by JAX's collectives and lax.ppermute only.
A program may use at most 128 MiB of HBM per device.

```python
import math
import jax
import jax.numpy as jnp
from jax import lax

BOX = 64
CAPB = 4
NORB = 16
PAIR_MEAN = 3
MOSTP = 4
SHIFT = 8
N_GRID = 8
N_PAIR = 4


def draw_pair_slots(key, part):
    worker_total = N_GRID * N_PAIR
    worker_keys = jax.random.split(jax.random.fold_in(key, 7), worker_total)

    def one_order(worker_key):
        return jax.random.permutation(worker_key, CAPB).astype(jnp.int32)
    orders = jax.vmap(one_order)(worker_keys)
    leading = orders.reshape(worker_total, CAPB // 2, 2)
    remaining = jax.random.randint(jax.random.fold_in(key, 8), (worker_total, MOSTP - CAPB // 2, 2), 0, CAPB, dtype=jnp.int32)
    joined = jnp.concatenate([leading, remaining], axis=1)
    return joined.reshape(N_GRID, N_PAIR, MOSTP, 2).astype(jnp.int32)


def draw_pair_count(key, part):
    floor_count = CAPB // 2
    highest = MOSTP - floor_count
    spare = N_PAIR * (PAIR_MEAN - floor_count) - highest
    worker_ids = jnp.arange(N_PAIR, dtype=jnp.int32)

    def one_row(row_id):
        row_key = jax.random.fold_in(jax.random.fold_in(key, 11), row_id)
        chosen = jax.random.randint(jax.random.fold_in(row_key, 1), (), 0, N_PAIR, dtype=jnp.int32)
        offset_pick = jax.random.randint(jax.random.fold_in(row_key, 2), (), 0, N_PAIR - 1, dtype=jnp.int32)
        spare_units = jnp.arange(spare, dtype=jnp.int32)
        ranked = (offset_pick + spare_units) % (N_PAIR - 1)
        target = ranked + (ranked >= chosen).astype(jnp.int32)
        extra_pairs = jnp.sum((target[:, None] == worker_ids[None, :]).astype(jnp.int32), axis=0)
        extra_pairs = jnp.where(worker_ids == chosen, highest, extra_pairs)
        return (floor_count + extra_pairs).astype(jnp.int32)
    row_ids = jnp.arange(N_GRID, dtype=jnp.int32)
    return jax.vmap(one_row)(row_ids).astype(jnp.int32)


def set_ends(values, key, least, largest):
    shape = values.shape
    place = [jax.random.randint(jax.random.fold_in(key, axis), (), 0, shape[axis]) for axis in range(len(shape))]
    values = values.at[tuple(place)].set(least)
    longest = shape.index(max(shape))
    place[longest] = (place[longest] + 1) % shape[longest]
    return values.at[tuple(place)].set(largest)


def block_levels(rng, shape, cuts, low, high):
    level = 1.0
    for position, parts in cuts:
        steps = jax.random.uniform(jax.random.fold_in(jax.random.fold_in(rng, 6), position), (parts,), jnp.float32, low / len(cuts), high / len(cuts))
        level = level * jnp.repeat(jnp.exp(steps), shape[position] // parts).reshape((-1,) + (1,) * (len(shape) - 1 - position))
    return level


def different_ones(rng, rows, amount, top, lift):
    order = jax.random.permutation(jax.random.fold_in(rng, 1), amount)
    boost = order
    for power in range(3):
        boost = boost * boost // amount
    boost = boost * lift // amount
    tickets = jax.random.randint(jax.random.fold_in(rng, 2), (rows, amount), 0, 4096) + boost
    sure = jax.random.permutation(jax.random.fold_in(rng, 3), rows)[jnp.arange(amount) % rows]
    tickets = jnp.where(jnp.arange(rows)[:, None] == sure[None, :], 1 << 14, tickets)
    score = tickets * amount + jnp.arange(amount)
    return lax.top_k(score.astype(jnp.int32), top)[1].astype(jnp.int32)


def gaussian(rng, dims, deviation, most, pieces=(), held_as=jnp.bfloat16):
    entries = deviation * jax.random.normal(rng, dims, jnp.float32)
    if pieces:
        entries = entries * block_levels(rng, dims, pieces, -0.22, 0.18)
    return jnp.clip(entries, -most, most).astype(held_as)


def setup_inputs(seed: int = 0) -> dict:
    splits = jax.random.split(jax.random.key(seed), 6)
    return {
        "orbitals": gaussian(splits[0], (BOX, NORB, BOX * BOX), 1.0, 6.0, ((0, 8), (2, 4))),
        "box_list": different_ones(splits[1], N_GRID * N_PAIR, NORB, CAPB, 2048).reshape((N_GRID, N_PAIR, CAPB)),
        "pair_slots": draw_pair_slots(jax.random.fold_in(splits[5], 71), 0),
        "offsets": set_ends(jax.random.randint(splits[3], (N_GRID, N_PAIR, MOSTP, 3), -SHIFT, SHIFT + 1), jax.random.fold_in(splits[3], 1), -SHIFT, SHIFT).astype(jnp.int32),
        "pair_count": draw_pair_count(jax.random.fold_in(splits[5], 71), 0),
    }


screening = 0.02


def cas_table(extent):
    places = jnp.arange(extent, dtype=jnp.int32)
    product = (places[:, None] * places[None, :]) % extent
    phases = product.astype(jnp.float32) * (2.0 * math.pi / extent)
    return jnp.cos(phases) + jnp.sin(phases)


def green_table(extent):
    phases = jnp.arange(extent, dtype=jnp.int32).astype(jnp.float32) * (2.0 * math.pi / extent)
    eigen = 2.0 - 2.0 * jnp.cos(phases)
    denominator = screening + eigen[:, None, None] + eigen[None, :, None] + eigen[None, None, :]
    return 1.0 / (denominator * float(extent ** 3))


def poisson(density, table, green):
    high = lax.Precision.HIGHEST
    spectrum = jnp.einsum("ax,xyz->ayz", table, density, precision=high)
    spectrum = jnp.einsum("by,ayz->abz", table, spectrum, precision=high)
    spectrum = jnp.einsum("cz,abz->abc", table, spectrum, precision=high)
    spectrum = spectrum * green
    spectrum = jnp.einsum("ax,xyz->ayz", table, spectrum, precision=high)
    spectrum = jnp.einsum("by,ayz->abz", table, spectrum, precision=high)
    return jnp.einsum("cz,abz->abc", table, spectrum, precision=high)


def shift_box(field, step_x, step_y, step_z):
    extent = field.shape[0]
    padded = jnp.pad(field, SHIFT)
    starts = (SHIFT + step_x, SHIFT + step_y, SHIFT + step_z)
    return lax.dynamic_slice(padded, starts, (extent, extent, extent))


def worker_fields(box_data, slot_list, offset_list, pair_total):
    extent = box_data.shape[0]
    capacity = box_data.shape[1]
    table = cas_table(extent)
    green = green_table(extent)

    def fetch(slot):
        picked = lax.dynamic_index_in_dim(box_data, slot, 1, False)
        return picked.astype(jnp.float32).reshape(extent, extent, extent)

    def add_slot(collected, slot, value):
        current = lax.dynamic_index_in_dim(collected, slot, 1, True)
        updated = current + value.reshape(extent, 1, extent * extent)
        return lax.dynamic_update_index_in_dim(collected, updated, slot, 1)

    def one_pair(turn, collected):
        first_slot = slot_list[turn, 0]
        second_slot = slot_list[turn, 1]
        offset = offset_list[turn]
        first_box = fetch(first_slot)
        second_box = fetch(second_slot)
        shifted = shift_box(second_box, offset[0], offset[1], offset[2])
        potential = poisson(first_box * shifted, table, green)
        collected = add_slot(collected, first_slot, -(potential * shifted))
        returned = shift_box(-(potential * first_box), -offset[0], -offset[1], -offset[2])
        return add_slot(collected, second_slot, returned)

    start = jnp.zeros((extent, capacity, extent * extent), jnp.float32)
    collected = lax.fori_loop(jnp.int32(0), pair_total.astype(jnp.int32), one_pair, start)
    return collected.astype(jnp.bfloat16)


def reference(orbitals, box_list, pair_slots, offsets, pair_count):
    extent = orbitals.shape[0]
    capacity = box_list.shape[2]
    workers = box_list.shape[0] * box_list.shape[1]
    lists = box_list.reshape(workers, capacity)
    slot_lists = pair_slots.reshape(workers, pair_slots.shape[2], 2)
    offset_lists = offsets.reshape(workers, offsets.shape[2], 3)
    totals = pair_count.reshape(workers)

    def visit(summed, worker_items):
        orbital_ids, slot_list, offset_list, pair_total = worker_items
        box_data = jnp.take(orbitals, orbital_ids, axis=1)
        fields = worker_fields(box_data, slot_list, offset_list, pair_total).astype(jnp.float32)
        return summed.at[:, orbital_ids, :].add(fields), None

    start = jnp.zeros((extent, orbitals.shape[1], extent * extent), jnp.float32)
    summed, _ = lax.scan(visit, start, (lists, slot_lists, offset_lists, totals))
    return summed
```

```python
import functools
import math

import jax
import jax.numpy as jnp
import ml_dtypes
import numpy as np
from jax import lax
from jax.experimental import pallas as pl
from jax.experimental.pallas import tpu as pltpu
from jax.sharding import PartitionSpec as P

SHIFT = 8
SCREENING = 0.02
F32 = jnp.float32
BF16 = jnp.bfloat16
VMEM_BYTES = 44 * 1024 * 1024


def split_np(values):
    high = values.astype(ml_dtypes.bfloat16)
    low = (values - high.astype(np.float64)).astype(ml_dtypes.bfloat16)
    return high, low


def stack_np(values, axis):
    high, low = split_np(values)
    return np.concatenate([high, high, low], axis=axis)


def tables(extent):
    half = extent // 2
    places = np.arange(extent)
    phases = (places[:, None] * places[None, :] % extent) * (2.0 * math.pi / extent)
    cas = np.cos(phases) + np.sin(phases)
    table_y = stack_np(cas, 1)
    parts = np.stack([cas[:half, xl::2] for xl in (0, 1)])
    ahead = stack_np(parts.reshape(extent, half), 1)
    back = stack_np(np.swapaxes(parts, 1, 2).reshape(extent, half), 1)
    butterfly = np.array([[1.0, 1.0], [1.0, -1.0]])
    table_z = stack_np(np.kron(butterfly, cas), 0)
    eigen = 2.0 - 2.0 * np.cos(places * (2.0 * math.pi / extent))
    denominator = SCREENING + eigen[:, None, None] + eigen[None, :, None] + eigen[None, None, :]
    green = -1.0 / (denominator * float(extent**3))
    green = green.reshape(2, half, extent, extent).transpose(2, 1, 0, 3)
    green = green.reshape(extent, half, 2 * extent).astype(np.float32)
    return table_y, ahead, back, table_z, green


def split(values):
    high = values.astype(BF16)
    return high, (values - high.astype(F32)).astype(BF16)


def three(values, axis):
    high, low = split(values)
    return jnp.concatenate([high, low, high], axis=axis)


def mul(left, right):
    return jnp.dot(left, right, preferred_element_type=F32)


def lane_low(extent):
    return lax.broadcasted_iota(jnp.int32, (1, 2 * extent), 1) < extent


def pieces_kernel(extent, slab, out, rows):
    planes, orbitals, cells = slab.shape
    heights = cells // extent
    wide = 2 * extent
    low = lane_low(extent)
    stride = (planes // 2) * heights
    for xh in range(planes // 2):
        for j in range(heights // 2):
            first = slab[2 * xh, :, j * wide : (j + 1) * wide].astype(F32)
            second = slab[2 * xh + 1, :, j * wide : (j + 1) * wide].astype(F32)
            even = jnp.where(low, first, pltpu.roll(second, extent, 1))
            odd = jnp.where(low, pltpu.roll(first, extent, 1), second)
            rows[pl.ds(xh * heights + 2 * j, orbitals, stride=stride), :] = even
            rows[pl.ds(xh * heights + 2 * j + 1, orbitals, stride=stride), :] = odd
    out[...] = rows[...].reshape(out.shape).astype(BF16)


def slab_kernel(extent, *refs):
    parts, out, rows = refs[:-2], refs[-2], refs[-1]
    planes, orbitals, cells = out.shape
    heights = cells // extent
    wide = 2 * extent
    low = lane_low(extent)
    stride = (planes // 2) * heights
    total = parts[0][...].astype(F32)
    for part in parts[1:]:
        total = total + part[...].astype(F32)
    rows[...] = total.reshape(rows.shape)
    for xh in range(planes // 2):
        for j in range(heights // 2):
            even = rows[pl.ds(xh * heights + 2 * j, orbitals, stride=stride), :]
            odd = rows[pl.ds(xh * heights + 2 * j + 1, orbitals, stride=stride), :]
            first = jnp.where(low, even, pltpu.roll(odd, extent, 1))
            second = jnp.where(low, pltpu.roll(even, extent, 1), odd)
            out[2 * xh, :, j * wide : (j + 1) * wide] = first
            out[2 * xh + 1, :, j * wide : (j + 1) * wide] = second


def choose_kernel(pair_total, grid_total, capacity, place, boxes, *refs):
    parts, outs = refs[:pair_total], refs[pair_total:]
    me, mate = place[0], place[1]
    for turn, out in enumerate(outs):
        target = lax.bitwise_xor(me, turn)
        for slot in range(capacity):
            orbital = boxes[(target * pair_total + mate) * capacity + slot]
            for step, part in enumerate(parts):
                out[slot, :, lax.bitwise_xor(mate, step)] = part[orbital]


def gather_kernel(pair_total, grid_total, capacity, place, boxes, *refs):
    parts, outs, total = refs[:grid_total], refs[grid_total:-1], refs[-1]
    me, mate = place[0], place[1]
    total[...] = jnp.zeros_like(total)
    for turn, part in enumerate(parts):
        origin = lax.bitwise_xor(me, turn)
        for slot in range(capacity):
            orbital = boxes[(origin * pair_total + mate) * capacity + slot]
            total[orbital] += part[slot].astype(F32)
    for step, out in enumerate(outs):
        out[...] = total[:, :, lax.bitwise_xor(mate, step)].astype(out.dtype)


def worker_kernel(extent, grid_total, place, slots, offsets, count, *refs):
    parts = refs[:grid_total]
    table_y, ahead, back, table_z, green = refs[grid_total : grid_total + 5]
    outs = refs[grid_total + 5 : 2 * grid_total + 5]
    box, shifted, first, second, returned, collected = refs[2 * grid_total + 5 :]
    capacity, local, pair_total, heights, wide = parts[0].shape
    half = extent // 2
    edge = SHIFT // 2
    me = place[0]
    low = lane_low(extent)
    lanes = lax.broadcasted_iota(jnp.int32, (1, wide), 1)
    depth = lanes - jnp.where(low, 0, extent)

    def clear(ref):
        blank = jnp.zeros((SHIFT, wide), F32)
        def one(index, carry):
            ref[index, :SHIFT] = blank
            ref[index, SHIFT + extent :] = blank
            return carry
        lax.fori_loop(0, ref.shape[0], one, 0)
        for index in (*range(edge), *range(edge + half, ref.shape[0])):
            ref[index] = jnp.zeros(ref.shape[1:], F32)

    clear(returned)
    for slot in range(capacity):
        clear(box.at[slot])
    for turn, part in enumerate(parts):
        start = edge + lax.bitwise_xor(me, turn) * local
        for slot in range(capacity):
            for xh in range(local):
                for p in range(pair_total):
                    box[slot, start + xh, SHIFT + p * heights : SHIFT + (p + 1) * heights] = part[
                        slot, xh, p
                    ].astype(F32)

    def moved(ref, xh, steps):
        step_x, step_y, step_z = steps
        odd = lax.bitwise_and(step_x, 1)
        near = edge + xh + lax.shift_right_arithmetic(step_x, 1)
        rows = pl.ds(SHIFT + step_y, extent)
        upper = ref[near, rows, :]
        lower = ref[near + odd, rows, :]
        joined = jnp.where(low, lower, upper)
        amount = lax.rem(2 * wide - odd * extent - step_z, wide)
        rolled = pltpu.roll(joined, amount, 1)
        kept = jnp.logical_and(depth + step_z >= 0, depth + step_z < extent)
        return jnp.where(kept, rolled, 0.0)

    def one_pair(turn, fresh):
        slot_a, slot_b = slots[2 * turn], slots[2 * turn + 1]
        steps = tuple(offsets[3 * turn + i] for i in range(3))
        opposite = tuple(-s for s in steps)

        def load_y(group, carry):
            for pair in range(2):
                stacks = []
                for member in range(2):
                    xh = group * 4 + pair * 2 + member
                    other = moved(box.at[slot_b], xh, steps)
                    shifted[xh] = other
                    own = box[slot_a, edge + xh, SHIFT : SHIFT + extent]
                    stacks.append(three(own * other, 0))
                done = mul(table_y[...], jnp.concatenate(stacks, axis=1))
                for member in range(2):
                    xh = group * 4 + pair * 2 + member
                    first[pl.ds(pl.multiple_of(xh * extent, extent), extent), :] = done[
                        :, member * wide : (member + 1) * wide
                    ]
            return carry

        lax.fori_loop(0, half // 4, load_y, 0)

        many = 8

        def middle(group, carry):
            def apply_x(table, values):
                results = []
                for pair in range(many // 2):
                    stack = jnp.concatenate([three(v, 0) for v in values[2 * pair : 2 * pair + 2]], axis=1)
                    done = mul(table[...], stack)
                    for member in range(2):
                        piece = done[:, member * wide : (member + 1) * wide]
                        results.append(jnp.where(low, piece[:half], piece[half:]))
                return results

            values = [
                first[pl.ds(group * many + i, half, stride=extent), :] for i in range(many)
            ]
            spectrum = jnp.concatenate(apply_x(ahead, values), axis=0)
            spectrum = mul(three(spectrum, 1), table_z[...])
            weights = green[pl.ds(group * many, many)].reshape(many * half, wide)
            spectrum = mul(three(spectrum * weights, 1), table_z[...])
            values = [spectrum[i * half : (i + 1) * half] for i in range(many)]
            for i, value in enumerate(apply_x(back, values)):
                second[pl.ds(group * many + i, half, stride=extent), :] = value
            return carry

        lax.fori_loop(0, extent // many, middle, 0)

        def unload_y(group, carry):
            for pair in range(2):
                stacks = []
                for member in range(2):
                    xh = group * 4 + pair * 2 + member
                    rows = pl.ds(pl.multiple_of(xh * extent, extent), extent)
                    stacks.append(three(second[rows, :], 0))
                done = mul(table_y[...], jnp.concatenate(stacks, axis=1))
                for member in range(2):
                    xh = group * 4 + pair * 2 + member
                    potential = done[:, member * wide : (member + 1) * wide]
                    value = potential * shifted[xh]
                    if fresh:
                        collected[slot_a, xh] = value
                    else:
                        collected[slot_a, xh] += value
                    own = box[slot_a, edge + xh, SHIFT : SHIFT + extent]
                    returned[edge + xh, SHIFT : SHIFT + extent] = potential * own
            return carry

        lax.fori_loop(0, half // 4, unload_y, 0)

        def give(group, carry):
            for member in range(4):
                xh = group * 4 + member
                value = moved(returned, xh, opposite)
                if fresh:
                    collected[slot_b, xh] = value
                else:
                    collected[slot_b, xh] += value
            return carry

        lax.fori_loop(0, half // 4, give, 0)

    def opening(turn, carry):
        one_pair(turn, True)
        return carry

    def later(turn, carry):
        one_pair(turn, False)
        return carry

    lax.fori_loop(0, capacity // 2, opening, 0)
    lax.fori_loop(capacity // 2, count[0], later, 0)

    for turn, out in enumerate(outs):
        start = lax.bitwise_xor(me, turn) * local
        for slot in range(capacity):
            for xh in range(local):
                for p in range(pair_total):
                    out[slot, xh, p] = collected[
                        slot, start + xh, p * heights : (p + 1) * heights
                    ].astype(BF16)


def spec(count):
    return [pl.BlockSpec(memory_space=pltpu.VMEM)] * count


def scalars(count):
    return [pl.BlockSpec(memory_space=pltpu.SMEM)] * count


def call(kernel, scalar_count, inputs, out_shapes, scratch, flops=0):
    moved = sum(math.prod(a.shape) * a.dtype.itemsize for a in (*inputs, *out_shapes))
    return pl.pallas_call(
        kernel,
        out_shape=out_shapes,
        in_specs=scalars(scalar_count) + spec(len(inputs) - scalar_count),
        out_specs=spec(len(out_shapes)),
        scratch_shapes=scratch,
        compiler_params=pltpu.CompilerParams(vmem_limit_bytes=VMEM_BYTES),
        cost_estimate=pl.CostEstimate(flops=flops, bytes_accessed=moved, transcendentals=0),
    )(*inputs)


def swap(arrays, axis, total):
    return [
        array if k == 0 else lax.ppermute(array, axis, [(i, i ^ k) for i in range(total)])
        for k, array in enumerate(arrays)
    ]


def shards(grid_total, pair_total, orbitals, box_list, pair_slots, offsets, pair_count):
    planes, orbital_total, cells = orbitals.shape
    capacity = box_list.shape[2]
    extent = planes * grid_total
    heights = cells // extent
    local, half, wide = planes // 2, extent // 2, 2 * extent
    padded_x, padded_y = half + SHIFT + 1, extent + 2 * SHIFT
    place = jnp.stack([lax.axis_index("grid"), lax.axis_index("pair")]).astype(jnp.int32)
    boxes = box_list.reshape(-1)
    shape = jax.ShapeDtypeStruct

    piece = (orbital_total, local, heights, wide)
    rows = pltpu.VMEM((math.prod(piece[:-1]), wide), F32)
    bundle = (capacity, local, pair_total, heights, wide)

    (own,) = call(functools.partial(pieces_kernel, extent), 0, [orbitals], [shape(piece, BF16)], [rows])
    gathered = swap([own] * pair_total, "pair", pair_total)
    outgoing = call(
        functools.partial(choose_kernel, pair_total, grid_total, capacity),
        2,
        [place, boxes, *gathered],
        [shape(bundle, BF16)] * grid_total,
        [],
    )
    arrived = swap(outgoing, "grid", grid_total)
    fields = call(
        functools.partial(worker_kernel, extent, grid_total),
        4,
        [
            place,
            pair_slots.reshape(-1),
            offsets.reshape(-1),
            pair_count.reshape(-1),
            *arrived,
            *(jnp.asarray(t) for t in tables(extent)),
        ],
        [shape(bundle, BF16)] * grid_total,
        [
            pltpu.VMEM((capacity, padded_x, padded_y, wide), F32),
            pltpu.VMEM((half, extent, wide), F32),
            pltpu.VMEM((half * extent, wide), F32),
            pltpu.VMEM((half * extent, wide), F32),
            pltpu.VMEM((padded_x, padded_y, wide), F32),
            pltpu.VMEM((capacity, half, extent, wide), F32),
        ],
        flops=3 * 2 * 6 * 3 * extent**4,
    )
    landed = swap(fields, "grid", grid_total)
    sums = call(
        functools.partial(gather_kernel, pair_total, grid_total, capacity),
        2,
        [place, boxes, *landed],
        [shape(piece, F32)] + [shape(piece, BF16)] * (pair_total - 1),
        [pltpu.VMEM((orbital_total, local, pair_total, heights, wide), F32)],
    )
    parts = swap(sums, "pair", pair_total)
    (result,) = call(
        functools.partial(slab_kernel, extent), 0, parts, [shape(orbitals.shape, F32)], [rows]
    )
    return result


def solution(mesh):
    placed = (
        P("grid", None, "pair"),
        P(),
        P("grid", "pair", None, None),
        P("grid", "pair", None, None),
        P("grid", "pair"),
    )
    body = functools.partial(shards, mesh.shape["grid"], mesh.shape["pair"])
    return jax.shard_map(
        body, mesh=mesh, in_specs=placed, out_specs=P("grid", None, "pair"), check_vma=False
    )
```

```python
import functools
import math

import jax
import jax.numpy as jnp
import ml_dtypes
import numpy as np
from jax import lax
from jax.experimental import pallas as pl
from jax.experimental.pallas import tpu as pltpu
from jax.sharding import PartitionSpec as P

SHIFT = 8
SCREENING = 0.02
F32 = jnp.float32
BF16 = jnp.bfloat16
CHOOSE_HINT = 60 * 10**9
VMEM_BYTES = 44 * 1024 * 1024


def split_np(values):
    high = values.astype(ml_dtypes.bfloat16)
    low = (values - high.astype(np.float64)).astype(ml_dtypes.bfloat16)
    return high, low


def stack_np(values, axis):
    high, low = split_np(values)
    return np.concatenate([high, high, low], axis=axis)


def tables(extent):
    half = extent // 2
    places = np.arange(extent)
    phases = (places[:, None] * places[None, :] % extent) * (2.0 * math.pi / extent)
    cas = np.cos(phases) + np.sin(phases)
    table_y = stack_np(cas, 1)
    parts = np.stack([cas[:half, xl::2] for xl in (0, 1)])
    ahead = stack_np(parts.reshape(extent, half), 1)
    back = stack_np(np.swapaxes(parts, 1, 2).reshape(extent, half), 1)
    butterfly = np.array([[1.0, 1.0], [1.0, -1.0]])
    table_z = stack_np(np.kron(butterfly, cas), 0)
    eigen = 2.0 - 2.0 * np.cos(places * (2.0 * math.pi / extent))
    denominator = SCREENING + eigen[:, None, None] + eigen[None, :, None] + eigen[None, None, :]
    green = -1.0 / (denominator * float(extent**3))
    green = green.reshape(2, half, extent, extent).transpose(2, 1, 0, 3)
    green = green.reshape(extent, half, 2 * extent).astype(np.float32)
    return table_y, ahead, back, table_z, green


def split(values):
    high = values.astype(BF16)
    return high, (values - high.astype(F32)).astype(BF16)


def three(values, axis):
    high, low = split(values)
    return jnp.concatenate([high, low, high], axis=axis)


def mul(left, right):
    return jnp.dot(left, right, preferred_element_type=F32)


def lane_low(extent):
    return lax.broadcasted_iota(jnp.int32, (1, 2 * extent), 1) < extent


def pieces_kernel(extent, slab, out, rows):
    planes, orbitals, cells = slab.shape
    heights = cells // extent
    wide = 2 * extent
    low = lane_low(extent)
    stride = (planes // 2) * heights
    for xh in range(planes // 2):
        for j in range(heights // 2):
            first = slab[2 * xh, :, j * wide : (j + 1) * wide].astype(F32)
            second = slab[2 * xh + 1, :, j * wide : (j + 1) * wide].astype(F32)
            even = jnp.where(low, first, pltpu.roll(second, extent, 1))
            odd = jnp.where(low, pltpu.roll(first, extent, 1), second)
            rows[pl.ds(xh * heights + 2 * j, orbitals, stride=stride), :] = even
            rows[pl.ds(xh * heights + 2 * j + 1, orbitals, stride=stride), :] = odd
    out[...] = rows[...].reshape(out.shape).astype(BF16)


def slab_kernel(extent, *refs):
    parts, out, rows = refs[:-2], refs[-2], refs[-1]
    planes, orbitals, cells = out.shape
    heights = cells // extent
    wide = 2 * extent
    low = lane_low(extent)
    stride = (planes // 2) * heights
    total = parts[0][...].astype(F32)
    for part in parts[1:]:
        total = total + part[...].astype(F32)
    rows[...] = total.reshape(rows.shape)
    for xh in range(planes // 2):
        for j in range(heights // 2):
            even = rows[pl.ds(xh * heights + 2 * j, orbitals, stride=stride), :]
            odd = rows[pl.ds(xh * heights + 2 * j + 1, orbitals, stride=stride), :]
            first = jnp.where(low, even, pltpu.roll(odd, extent, 1))
            second = jnp.where(low, pltpu.roll(even, extent, 1), odd)
            out[2 * xh, :, j * wide : (j + 1) * wide] = first
            out[2 * xh + 1, :, j * wide : (j + 1) * wide] = second


def choose_kernel(pair_total, capacity, place, boxes, *refs):
    parts, outs = refs[:-1], refs[-1]
    mate = place[1]
    for target in range(outs.shape[0]):
        for slot in range(capacity):
            orbital = boxes[(target * pair_total + mate) * capacity + slot]
            for step, part in enumerate(parts):
                outs[target, slot, :, step] = part[orbital]


def gather_kernel(pair_total, capacity, place, boxes, landed, *refs):
    outs, total = refs[:-1], refs[-1]
    mate = place[1]
    total[...] = jnp.zeros_like(total)
    for origin in range(landed.shape[0]):
        for slot in range(capacity):
            orbital = boxes[(origin * pair_total + mate) * capacity + slot]
            total[orbital] += landed[origin, slot].astype(F32)
    for step, out in enumerate(outs):
        out[...] = total[:, :, step].astype(out.dtype)


def worker_kernel(extent, place, slots, offsets, count, *refs):
    parts = refs[:2]
    table_y, ahead, back, table_z, green = refs[2:7]
    outs = refs[7:9]
    box, shifted, first, second, returned, collected = refs[9:]
    grid_total, capacity, local, _, heights, wide = parts[0].shape
    mate = place[1]
    half = extent // 2
    edge = SHIFT // 2
    low = lane_low(extent)
    lanes = lax.broadcasted_iota(jnp.int32, (1, wide), 1)
    depth = lanes - jnp.where(low, 0, extent)

    def clear(ref):
        blank = jnp.zeros((SHIFT, wide), F32)
        def one(index, carry):
            ref[index, :SHIFT] = blank
            ref[index, SHIFT + extent :] = blank
            return carry
        lax.fori_loop(0, ref.shape[0], one, 0)
        for index in (*range(edge), *range(edge + half, ref.shape[0])):
            ref[index] = jnp.zeros(ref.shape[1:], F32)

    clear(returned)
    for slot in range(capacity):
        clear(box.at[slot])
    def all_rows(visit):
        step = 0
        for chunk, part in enumerate(parts):
            for index in range(part.shape[3]):
                row = lax.bitwise_xor(mate, step) * heights
                step += 1
                for origin in range(grid_total):
                    for slot in range(capacity):
                        for xh in range(local):
                            visit(chunk, (origin, slot, xh, index), slot, origin * local + xh, row)

    def fill(chunk, index, slot, xh, row):
        rows = pl.ds(pl.multiple_of(SHIFT + row, 8), heights)
        box[slot, edge + xh, rows] = parts[chunk][index].astype(F32)

    all_rows(fill)

    def moved(ref, xh, steps):
        step_x, step_y, step_z = steps
        odd = lax.bitwise_and(step_x, 1)
        near = edge + xh + lax.shift_right_arithmetic(step_x, 1)
        rows = pl.ds(SHIFT + step_y, extent)
        upper = ref[near, rows, :]
        lower = ref[near + odd, rows, :]
        joined = jnp.where(low, lower, upper)
        amount = lax.rem(2 * wide - odd * extent - step_z, wide)
        rolled = pltpu.roll(joined, amount, 1)
        kept = jnp.logical_and(depth + step_z >= 0, depth + step_z < extent)
        return jnp.where(kept, rolled, 0.0)

    def one_pair(turn, fresh):
        slot_a, slot_b = slots[2 * turn], slots[2 * turn + 1]
        steps = tuple(offsets[3 * turn + i] for i in range(3))
        opposite = tuple(-s for s in steps)

        def load_y(group, carry):
            for pair in range(16):
                stacks = []
                for member in range(2):
                    xh = group * 32 + pair * 2 + member
                    other = moved(box.at[slot_b], xh, steps)
                    shifted[xh] = other
                    own = box[slot_a, edge + xh, SHIFT : SHIFT + extent]
                    stacks.append(three(own * other, 0))
                done = mul(table_y[...], jnp.concatenate(stacks, axis=1))
                for member in range(2):
                    xh = group * 32 + pair * 2 + member
                    first[pl.ds(pl.multiple_of(xh * extent, extent), extent), :] = done[
                        :, member * wide : (member + 1) * wide
                    ]
            return carry

        lax.fori_loop(0, half // 32, load_y, 0)

        many = 64

        def middle(group, carry):
            def apply_x(table, values):
                results = []
                for pair in range(many // 2):
                    stack = jnp.concatenate([three(v, 0) for v in values[2 * pair : 2 * pair + 2]], axis=1)
                    done = mul(table[...], stack)
                    for member in range(2):
                        piece = done[:, member * wide : (member + 1) * wide]
                        results.append(jnp.where(low, piece[:half], piece[half:]))
                return results

            values = [
                first[pl.ds(group * many + i, half, stride=extent), :] for i in range(many)
            ]
            spectrum = jnp.concatenate(apply_x(ahead, values), axis=0)
            spectrum = mul(three(spectrum, 1), table_z[...])
            weights = green[pl.ds(group * many, many)].reshape(many * half, wide)
            spectrum = mul(three(spectrum * weights, 1), table_z[...])
            values = [spectrum[i * half : (i + 1) * half] for i in range(many)]
            for i, value in enumerate(apply_x(back, values)):
                second[pl.ds(group * many + i, half, stride=extent), :] = value
            return carry

        lax.fori_loop(0, extent // many, middle, 0)

        def unload_y(group, carry):
            for pair in range(16):
                stacks = []
                for member in range(2):
                    xh = group * 32 + pair * 2 + member
                    rows = pl.ds(pl.multiple_of(xh * extent, extent), extent)
                    stacks.append(three(second[rows, :], 0))
                done = mul(table_y[...], jnp.concatenate(stacks, axis=1))
                for member in range(2):
                    xh = group * 32 + pair * 2 + member
                    potential = done[:, member * wide : (member + 1) * wide]
                    value = potential * shifted[xh]
                    if fresh:
                        collected[slot_a, xh] = value
                    else:
                        collected[slot_a, xh] += value
                    own = box[slot_a, edge + xh, SHIFT : SHIFT + extent]
                    returned[edge + xh, SHIFT : SHIFT + extent] = potential * own
            return carry

        lax.fori_loop(0, half // 32, unload_y, 0)

        def give(group, carry):
            for member in range(32):
                xh = group * 32 + member
                value = moved(returned, xh, opposite)
                if fresh:
                    collected[slot_b, xh] = value
                else:
                    collected[slot_b, xh] += value
            return carry

        lax.fori_loop(0, half // 32, give, 0)

    def opening(turn, carry):
        one_pair(turn, True)
        return carry

    def later(turn, carry):
        one_pair(turn, False)
        return carry

    lax.fori_loop(0, capacity // 2, opening, 0)
    lax.fori_loop(capacity // 2, count[0], later, 0)

    def empty(chunk, index, slot, xh, row):
        rows = pl.ds(pl.multiple_of(row, 8), heights)
        outs[chunk][index] = collected[slot, xh, rows].astype(BF16)

    all_rows(empty)


def spec(count):
    return [pl.BlockSpec(memory_space=pltpu.VMEM)] * count


def scalars(count):
    return [pl.BlockSpec(memory_space=pltpu.SMEM)] * count


def call(kernel, scalar_count, inputs, out_shapes, scratch, flops=0):
    moved = sum(math.prod(a.shape) * a.dtype.itemsize for a in (*inputs, *out_shapes))
    return pl.pallas_call(
        kernel,
        out_shape=out_shapes,
        in_specs=scalars(scalar_count) + spec(len(inputs) - scalar_count),
        out_specs=spec(len(out_shapes)),
        scratch_shapes=scratch,
        compiler_params=pltpu.CompilerParams(vmem_limit_bytes=VMEM_BYTES),
        cost_estimate=pl.CostEstimate(flops=flops, bytes_accessed=moved, transcendentals=0),
    )(*inputs)


def worker_call(extent, place, slots, offsets, count, arrived, constants):
    capacity = arrived[0].shape[1]
    half, wide = extent // 2, 2 * extent
    padded_x, padded_y = half + SHIFT + 1, extent + 2 * SHIFT
    return call(
        functools.partial(worker_kernel, extent),
        4,
        [place, slots, offsets, count, *arrived, *constants],
        [jax.ShapeDtypeStruct(a.shape, BF16) for a in arrived],
        [
            pltpu.VMEM((capacity, padded_x, padded_y, wide), F32),
            pltpu.VMEM((half, extent, wide), F32),
            pltpu.VMEM((half * extent, wide), F32),
            pltpu.VMEM((half * extent, wide), F32),
            pltpu.VMEM((padded_x, padded_y, wide), F32),
            pltpu.VMEM((capacity, half, extent, wide), F32),
        ],
        flops=3 * 2 * 6 * 3 * extent**4,
    )


def over_pair(array, step, total):
    return array if step == 0 else lax.ppermute(array, "pair", [(i, i ^ step) for i in range(total)])


def over_grid(array):
    return lax.all_to_all(array, "grid", 0, 0, tiled=True)


def shards(grid_total, pair_total, orbitals, box_list, pair_slots, offsets, pair_count):
    planes, orbital_total, cells = orbitals.shape
    capacity = box_list.shape[2]
    extent = planes * grid_total
    heights = cells // extent
    local, wide = planes // 2, 2 * extent
    place = jnp.stack([lax.axis_index("grid"), lax.axis_index("pair")]).astype(jnp.int32)
    boxes = box_list.reshape(-1)
    shape = jax.ShapeDtypeStruct
    chunks = (range(pair_total // 2), range(pair_total // 2, pair_total))

    piece = (orbital_total, local, heights, wide)
    rows = pltpu.VMEM((math.prod(piece[:-1]), wide), F32)

    (own,) = call(functools.partial(pieces_kernel, extent), 0, [orbitals], [shape(piece, BF16)], [rows])
    gathered = [over_pair(own, step, pair_total) for step in range(pair_total)]
    arrived = []
    for chunk in chunks:
        bundle = (grid_total, capacity, local, len(chunk), heights, wide)
        (outgoing,) = call(
            functools.partial(choose_kernel, pair_total, capacity),
            2,
            [place, boxes, *(gathered[step] for step in chunk)],
            [shape(bundle, BF16)],
            [],
            flops=CHOOSE_HINT,
        )
        arrived.append(over_grid(outgoing))
    fields = worker_call(
        extent,
        place,
        pair_slots.reshape(-1),
        offsets.reshape(-1),
        pair_count.reshape(-1),
        arrived,
        [jnp.asarray(t) for t in tables(extent)],
    )
    parts = [None] * pair_total
    for chunk, field in reversed(list(zip(chunks, fields))):
        sums = call(
            functools.partial(gather_kernel, pair_total, capacity),
            2,
            [place, boxes, over_grid(field)],
            [shape(piece, F32 if step == 0 else BF16) for step in chunk],
            [pltpu.VMEM((orbital_total, local, len(chunk), heights, wide), F32)],
        )
        for step, value in zip(chunk, sums):
            parts[step] = over_pair(value, step, pair_total)
    (result,) = call(
        functools.partial(slab_kernel, extent), 0, parts, [shape(orbitals.shape, F32)], [rows]
    )
    return result


def solution(mesh):
    placed = (
        P("grid", None, "pair"),
        P(),
        P("grid", "pair", None, None),
        P("grid", "pair", None, None),
        P("grid", "pair"),
    )
    body = functools.partial(shards, mesh.shape["grid"], mesh.shape["pair"])
    return jax.shard_map(
        body, mesh=mesh, in_specs=placed, out_specs=P("grid", None, "pair"), check_vma=False
    )
```

```python
import functools
import math

import jax
import jax.numpy as jnp
import ml_dtypes
import numpy as np
from jax import lax
from jax.experimental import pallas as pl
from jax.experimental.pallas import tpu as pltpu
from jax.sharding import PartitionSpec as P

SHIFT = 8
SCREENING = 0.02
F32 = jnp.float32
BF16 = jnp.bfloat16
CHOOSE_HINT = (60 * 10**9, 60 * 10**9)
SPLIT_IN = (False, True)
SPLIT_OUT = (False, True)
VMEM_BYTES = 44 * 1024 * 1024


def split_np(values):
    high = values.astype(ml_dtypes.bfloat16)
    low = (values - high.astype(np.float64)).astype(ml_dtypes.bfloat16)
    return high, low


def stack_np(values, axis):
    high, low = split_np(values)
    return np.concatenate([high, high, low], axis=axis)


def tables(extent):
    half = extent // 2
    places = np.arange(extent)
    phases = (places[:, None] * places[None, :] % extent) * (2.0 * math.pi / extent)
    cas = np.cos(phases) + np.sin(phases)
    table_y = stack_np(cas, 1)
    parts = np.stack([cas[:half, xl::2] for xl in (0, 1)])
    ahead = stack_np(parts.reshape(extent, half), 1)
    back = stack_np(np.swapaxes(parts, 1, 2).reshape(extent, half), 1)
    butterfly = np.array([[1.0, 1.0], [1.0, -1.0]])
    table_z = stack_np(np.kron(butterfly, cas), 0)
    eigen = 2.0 - 2.0 * np.cos(places * (2.0 * math.pi / extent))
    denominator = SCREENING + eigen[:, None, None] + eigen[None, :, None] + eigen[None, None, :]
    green = -1.0 / (denominator * float(extent**3))
    green = green.reshape(2, half, extent, extent).transpose(2, 1, 0, 3)
    green = green.reshape(extent, half, 2 * extent).astype(np.float32)
    return table_y, ahead, back, table_z, green


def split(values):
    high = values.astype(BF16)
    return high, (values - high.astype(F32)).astype(BF16)


def three(values, axis):
    high, low = split(values)
    return jnp.concatenate([high, low, high], axis=axis)


def mul(left, right):
    return jnp.dot(left, right, preferred_element_type=F32)


def lane_low(extent):
    return lax.broadcasted_iota(jnp.int32, (1, 2 * extent), 1) < extent


def pieces_kernel(extent, slab, out, rows):
    planes, orbitals, cells = slab.shape
    heights = cells // extent
    wide = 2 * extent
    low = lane_low(extent)
    stride = (planes // 2) * heights
    for xh in range(planes // 2):
        for j in range(heights // 2):
            first = slab[2 * xh, :, j * wide : (j + 1) * wide].astype(F32)
            second = slab[2 * xh + 1, :, j * wide : (j + 1) * wide].astype(F32)
            even = jnp.where(low, first, pltpu.roll(second, extent, 1))
            odd = jnp.where(low, pltpu.roll(first, extent, 1), second)
            rows[pl.ds(xh * heights + 2 * j, orbitals, stride=stride), :] = even
            rows[pl.ds(xh * heights + 2 * j + 1, orbitals, stride=stride), :] = odd
    out[...] = rows[...].reshape(out.shape).astype(BF16)


def slab_kernel(extent, *refs):
    parts, out, rows = refs[:-2], refs[-2], refs[-1]
    planes, orbitals, cells = out.shape
    heights = cells // extent
    wide = 2 * extent
    low = lane_low(extent)
    stride = (planes // 2) * heights
    total = parts[0][...].astype(F32)
    for part in parts[1:]:
        total = total + part[...].astype(F32)
    rows[...] = total.reshape(rows.shape)
    for xh in range(planes // 2):
        for j in range(heights // 2):
            even = rows[pl.ds(xh * heights + 2 * j, orbitals, stride=stride), :]
            odd = rows[pl.ds(xh * heights + 2 * j + 1, orbitals, stride=stride), :]
            first = jnp.where(low, even, pltpu.roll(odd, extent, 1))
            second = jnp.where(low, pltpu.roll(even, extent, 1), odd)
            out[2 * xh, :, j * wide : (j + 1) * wide] = first
            out[2 * xh + 1, :, j * wide : (j + 1) * wide] = second


def partners(refs, me):
    if len(refs) == 1:
        return [(index, refs[0].at[index]) for index in range(refs[0].shape[0])]
    return [(lax.bitwise_xor(me, turn), ref) for turn, ref in enumerate(refs)]


def choose_kernel(pair_total, capacity, part_total, place, boxes, *refs):
    parts, outs = refs[:part_total], refs[part_total:]
    for target, out in partners(outs, place[0]):
        for slot in range(capacity):
            orbital = boxes[(target * pair_total + place[1]) * capacity + slot]
            for step, part in enumerate(parts):
                out[slot, :, step] = part[orbital]


def gather_kernel(pair_total, capacity, landed_total, place, boxes, *refs):
    landed, outs, total = refs[:landed_total], refs[landed_total:-1], refs[-1]
    total[...] = jnp.zeros_like(total)
    for origin, bundle in partners(landed, place[0]):
        for slot in range(capacity):
            orbital = boxes[(origin * pair_total + place[1]) * capacity + slot]
            total[orbital] += bundle[slot].astype(F32)
    for step, out in enumerate(outs):
        out[...] = total[:, :, step].astype(out.dtype)


def worker_kernel(extent, arrived_totals, sent_totals, place, slots, offsets, count, *refs):
    refs = list(refs)
    parts = [[refs.pop(0) for _ in range(total)] for total in arrived_totals]
    table_y, ahead, back, table_z, green = [refs.pop(0) for _ in range(5)]
    outs = [[refs.pop(0) for _ in range(total)] for total in sent_totals]
    box, shifted, first, second, returned, collected = refs
    capacity, local, _, heights, wide = parts[0][-1].shape[-5:]
    me, mate = place[0], place[1]
    half = extent // 2
    edge = SHIFT // 2
    low = lane_low(extent)
    lanes = lax.broadcasted_iota(jnp.int32, (1, wide), 1)
    depth = lanes - jnp.where(low, 0, extent)

    def clear(ref):
        blank = jnp.zeros((SHIFT, wide), F32)
        def one(index, carry):
            ref[index, :SHIFT] = blank
            ref[index, SHIFT + extent :] = blank
            return carry
        lax.fori_loop(0, ref.shape[0], one, 0)
        for index in (*range(edge), *range(edge + half, ref.shape[0])):
            ref[index] = jnp.zeros(ref.shape[1:], F32)

    clear(returned)
    for slot in range(capacity):
        clear(box.at[slot])
    def all_rows(lists, visit):
        step = 0
        for bundles in lists:
            for index in range(bundles[0].shape[-3]):
                row = lax.bitwise_xor(mate, step) * heights
                step += 1
                for origin, bundle in partners(bundles, me):
                    for slot in range(capacity):
                        for xh in range(local):
                            visit(bundle, (slot, xh, index), origin * local + xh, row)

    def fill(bundle, index, xh, row):
        rows = pl.ds(pl.multiple_of(SHIFT + row, 8), heights)
        box[index[0], edge + xh, rows] = bundle[index].astype(F32)

    all_rows(parts, fill)

    def moved(ref, xh, steps):
        step_x, step_y, step_z = steps
        odd = lax.bitwise_and(step_x, 1)
        near = edge + xh + lax.shift_right_arithmetic(step_x, 1)
        rows = pl.ds(SHIFT + step_y, extent)
        upper = ref[near, rows, :]
        lower = ref[near + odd, rows, :]
        joined = jnp.where(low, lower, upper)
        amount = lax.rem(2 * wide - odd * extent - step_z, wide)
        rolled = pltpu.roll(joined, amount, 1)
        kept = jnp.logical_and(depth + step_z >= 0, depth + step_z < extent)
        return jnp.where(kept, rolled, 0.0)

    def one_pair(turn, fresh):
        slot_a, slot_b = slots[2 * turn], slots[2 * turn + 1]
        steps = tuple(offsets[3 * turn + i] for i in range(3))
        opposite = tuple(-s for s in steps)

        def load_y(group, carry):
            for pair in range(16):
                stacks = []
                for member in range(2):
                    xh = group * 32 + pair * 2 + member
                    other = moved(box.at[slot_b], xh, steps)
                    shifted[xh] = other
                    own = box[slot_a, edge + xh, SHIFT : SHIFT + extent]
                    stacks.append(three(own * other, 0))
                done = mul(table_y[...], jnp.concatenate(stacks, axis=1))
                for member in range(2):
                    xh = group * 32 + pair * 2 + member
                    first[pl.ds(pl.multiple_of(xh * extent, extent), extent), :] = done[
                        :, member * wide : (member + 1) * wide
                    ]
            return carry

        lax.fori_loop(0, half // 32, load_y, 0)

        many = 64

        def middle(group, carry):
            def apply_x(table, values):
                results = []
                for pair in range(many // 2):
                    stack = jnp.concatenate([three(v, 0) for v in values[2 * pair : 2 * pair + 2]], axis=1)
                    done = mul(table[...], stack)
                    for member in range(2):
                        piece = done[:, member * wide : (member + 1) * wide]
                        results.append(jnp.where(low, piece[:half], piece[half:]))
                return results

            values = [
                first[pl.ds(group * many + i, half, stride=extent), :] for i in range(many)
            ]
            spectrum = jnp.concatenate(apply_x(ahead, values), axis=0)
            spectrum = mul(three(spectrum, 1), table_z[...])
            weights = green[pl.ds(group * many, many)].reshape(many * half, wide)
            spectrum = mul(three(spectrum * weights, 1), table_z[...])
            values = [spectrum[i * half : (i + 1) * half] for i in range(many)]
            for i, value in enumerate(apply_x(back, values)):
                second[pl.ds(group * many + i, half, stride=extent), :] = value
            return carry

        lax.fori_loop(0, extent // many, middle, 0)

        def unload_y(group, carry):
            for pair in range(16):
                stacks = []
                for member in range(2):
                    xh = group * 32 + pair * 2 + member
                    rows = pl.ds(pl.multiple_of(xh * extent, extent), extent)
                    stacks.append(three(second[rows, :], 0))
                done = mul(table_y[...], jnp.concatenate(stacks, axis=1))
                for member in range(2):
                    xh = group * 32 + pair * 2 + member
                    potential = done[:, member * wide : (member + 1) * wide]
                    value = potential * shifted[xh]
                    if fresh:
                        collected[slot_a, xh] = value
                    else:
                        collected[slot_a, xh] += value
                    own = box[slot_a, edge + xh, SHIFT : SHIFT + extent]
                    returned[edge + xh, SHIFT : SHIFT + extent] = potential * own
            return carry

        lax.fori_loop(0, half // 32, unload_y, 0)

        def give(group, carry):
            for member in range(32):
                xh = group * 32 + member
                value = moved(returned, xh, opposite)
                if fresh:
                    collected[slot_b, xh] = value
                else:
                    collected[slot_b, xh] += value
            return carry

        lax.fori_loop(0, half // 32, give, 0)

    def opening(turn, carry):
        one_pair(turn, True)
        return carry

    def later(turn, carry):
        one_pair(turn, False)
        return carry

    lax.fori_loop(0, capacity // 2, opening, 0)
    lax.fori_loop(capacity // 2, count[0], later, 0)

    def empty(bundle, index, xh, row):
        rows = pl.ds(pl.multiple_of(row, 8), heights)
        bundle[index] = collected[index[0], xh, rows].astype(BF16)

    all_rows(outs, empty)


def spec(count):
    return [pl.BlockSpec(memory_space=pltpu.VMEM)] * count


def scalars(count):
    return [pl.BlockSpec(memory_space=pltpu.SMEM)] * count


def call(kernel, scalar_count, inputs, out_shapes, scratch, flops=0):
    moved = sum(math.prod(a.shape) * a.dtype.itemsize for a in (*inputs, *out_shapes))
    return pl.pallas_call(
        kernel,
        out_shape=out_shapes,
        in_specs=scalars(scalar_count) + spec(len(inputs) - scalar_count),
        out_specs=spec(len(out_shapes)),
        scratch_shapes=scratch,
        compiler_params=pltpu.CompilerParams(vmem_limit_bytes=VMEM_BYTES),
        cost_estimate=pl.CostEstimate(flops=flops, bytes_accessed=moved, transcendentals=0),
    )(*inputs)


def worker_call(extent, place, slots, offsets, count, arrived, sent, constants):
    capacity = arrived[0][-1].shape[-5]
    half, wide = extent // 2, 2 * extent
    padded_x, padded_y = half + SHIFT + 1, extent + 2 * SHIFT
    return call(
        functools.partial(worker_kernel, extent, [len(a) for a in arrived], [len(s) for s in sent]),
        4,
        [place, slots, offsets, count, *arrived[0], *arrived[1], *constants],
        [*sent[0], *sent[1]],
        [
            pltpu.VMEM((capacity, padded_x, padded_y, wide), F32),
            pltpu.VMEM((half, extent, wide), F32),
            pltpu.VMEM((half * extent, wide), F32),
            pltpu.VMEM((half * extent, wide), F32),
            pltpu.VMEM((padded_x, padded_y, wide), F32),
            pltpu.VMEM((capacity, half, extent, wide), F32),
        ],
        flops=3 * 2 * 6 * 3 * extent**4,
    )


def over_pair(array, step, total):
    return array if step == 0 else lax.ppermute(array, "pair", [(i, i ^ step) for i in range(total)])


def over_grid(bundles, total):
    if len(bundles) == 1:
        return [lax.all_to_all(bundles[0], "grid", 0, 0, tiled=True)]
    return [
        bundle if turn == 0 else lax.ppermute(bundle, "grid", [(i, i ^ turn) for i in range(total)])
        for turn, bundle in enumerate(bundles)
    ]


def bundle_shapes(split_up, grid_total, single):
    if split_up:
        return [jax.ShapeDtypeStruct(single, BF16)] * grid_total
    return [jax.ShapeDtypeStruct((grid_total, *single), BF16)]


def shards(grid_total, pair_total, orbitals, box_list, pair_slots, offsets, pair_count):
    planes, orbital_total, cells = orbitals.shape
    capacity = box_list.shape[2]
    extent = planes * grid_total
    heights = cells // extent
    local, wide = planes // 2, 2 * extent
    place = jnp.stack([lax.axis_index("grid"), lax.axis_index("pair")]).astype(jnp.int32)
    boxes = box_list.reshape(-1)
    shape = jax.ShapeDtypeStruct
    chunks = (range(pair_total // 2), range(pair_total // 2, pair_total))

    piece = (orbital_total, local, heights, wide)
    rows = pltpu.VMEM((math.prod(piece[:-1]), wide), F32)

    (own,) = call(functools.partial(pieces_kernel, extent), 0, [orbitals], [shape(piece, BF16)], [rows])
    gathered = [over_pair(own, step, pair_total) for step in range(pair_total)]
    arrived, sent = [], []
    for chunk, split_in, split_out in zip(chunks, SPLIT_IN, SPLIT_OUT):
        single = (capacity, local, len(chunk), heights, wide)
        outgoing = call(
            functools.partial(choose_kernel, pair_total, capacity, len(chunk)),
            2,
            [place, boxes, *(gathered[step] for step in chunk)],
            bundle_shapes(split_in, grid_total, single),
            [],
            flops=CHOOSE_HINT[chunk[0] > 0],
        )
        arrived.append(over_grid(outgoing, grid_total))
        sent.append(bundle_shapes(split_out, grid_total, single))
    fields = worker_call(
        extent,
        place,
        pair_slots.reshape(-1),
        offsets.reshape(-1),
        pair_count.reshape(-1),
        arrived,
        sent,
        [jnp.asarray(t) for t in tables(extent)],
    )
    fields = (fields[: len(sent[0])], fields[len(sent[0]) :])
    parts = []
    for chunk, field in reversed(list(zip(chunks, fields))):
        if parts:
            field = lax.optimization_barrier((*field, *landed))[: len(field)]
        landed = over_grid(field, grid_total)
        sums = call(
            functools.partial(gather_kernel, pair_total, capacity, len(landed)),
            2,
            [place, boxes, *landed],
            [shape(piece, BF16 if step > 0 else F32) for step in chunk],
            [pltpu.VMEM((orbital_total, local, len(chunk), heights, wide), F32)],
        )
        parts += [over_pair(value, step, pair_total) for step, value in zip(chunk, sums)]
    (result,) = call(
        functools.partial(slab_kernel, extent), 0, parts, [shape(orbitals.shape, F32)], [rows]
    )
    return result


def solution(mesh):
    placed = (
        P("grid", None, "pair"),
        P(),
        P("grid", "pair", None, None),
        P("grid", "pair", None, None),
        P("grid", "pair"),
    )
    body = functools.partial(shards, mesh.shape["grid"], mesh.shape["pair"])
    return jax.shard_map(
        body, mesh=mesh, in_specs=placed, out_specs=P("grid", None, "pair"), check_vma=False
    )
```
